128 devices in a mesh: group: 8 (over y, core), index: 16 (over z, x).
Axes of the slice: x: 4, y: 4, z: 4, core: 2. Of those that a mesh axis runs over, the one named last changes fastest.
Arguments:
- acts: bfloat16 [8192, 4096], P(('group', 'index')), may hold values from -6 to 6
- enc_weight: bfloat16 [4096, 16384], P(None, 'index'), may hold values from -0.09375 to 0.09375
- enc_bias: float32 [16384], P('index'), may hold values from -3 to 3
- dec_weight: bfloat16 [16384, 4096], P('index'), may hold values from -0.1875 to 0.1875
- dec_bias: float32 [4096], replicated, may hold values from -3 to 3
- active: int32 [128, 32], P('group'), may hold values from 0 to 255, all different within a row
- counts: int32 [128], P('group'), may hold values from 1 to 32
Outputs:
- reconstruction: bfloat16 [8192, 4096], P(('group', 'index'))
- dec_grad: float32 [16384, 4096], P(('index', 'group'))
The draws below stay inside these ranges and needn't reach their ends.
Inputs may be any that keep to these rules, and one draw needn't show every extreme that they name: `active`: only the first counts[r] entries of row r are live; the entries of a row are distinct.
All inputs are finite; a program needn't handle non-finite values.
Results may differ from the reference program's by a relative error of at most 0.015.
Values may be sent and summed in bfloat16 or wider, within the bound.
No kernel may reach another device: no remote copies, remote signals or barrier semaphores. Data moves between devices by JAX's collectives and lax.ppermute only.
A program may use at most 128 MiB of HBM per device.

```python
import jax
import jax.numpy as jnp
from jax import lax

D = 4096
BLOCK = 64
KB = 32
LAT_DEV = 1024
TOK_DEV = 64
LATENTS = 16384
NBLK = 256
GROUP_ROWS = 1024
ROWBLOCKS = 128
TOKENS = 8192
N_GROUP = 8
N_INDEX = 16


def draw_counts(key, part):
    key = jax.random.fold_in(key, 11)
    values = jax.random.randint(key, (ROWBLOCKS,), 1, KB + 1)
    values = values.at[0].set(KB).at[1].set(1)
    return values.astype(jnp.int32)


def block_levels(key, shape, shards, least, largest):
    def one(position, blocks):
        draws = jax.random.uniform(jax.random.fold_in(jax.random.fold_in(key, 6), position), (blocks,), jnp.float32, least / len(shards), largest / len(shards))
        return jnp.repeat(jnp.exp(draws), shape[position] // blocks).reshape((-1,) + (1,) * (len(shape) - position - 1))

    loudness = one(*shards[0])
    for cut in shards[1:]:
        loudness = loudness * one(*cut)
    return loudness


def different_ones(stream_key, rows, number_of, top, lift):
    ranking = jax.random.permutation(jax.random.fold_in(stream_key, 1), number_of)
    pull = ranking
    for power in range(3):
        pull = pull * pull // number_of
    pull = pull * lift // number_of
    tickets = jax.random.randint(jax.random.fold_in(stream_key, 2), (rows, number_of), 0, 4096) + pull
    fixed_rows = jax.random.permutation(jax.random.fold_in(stream_key, 3), rows)[jnp.arange(number_of) % rows]
    tickets = jnp.where(jnp.arange(rows)[:, None] == fixed_rows[None, :], 1 << 14, tickets)
    merit = tickets * number_of + jnp.arange(number_of)
    return lax.top_k(merit.astype(jnp.int32), top)[1].astype(jnp.int32)


def normal_values(rng, dims, spread, reach, shards=(), held_as=jnp.bfloat16):
    factor_of = block_levels(rng, dims, shards, -0.22, 0.18) if shards else 1.0
    array = jax.random.normal(rng, dims, jnp.float32) * spread * factor_of
    return jnp.minimum(jnp.maximum(array, -reach), reach).astype(held_as)


def setup_inputs(seed: int = 0) -> dict:
    key_list = jax.random.split(jax.random.key(seed), 8)
    acts = normal_values(key_list[0], (TOKENS, D), 1.0, 6.0, ((0, 128),))
    enc_weight = normal_values(key_list[1], (D, LATENTS), D ** -0.5, 0.09375, ((1, 16),))
    enc_bias = normal_values(key_list[2], (LATENTS,), 0.5, 3.0, ((0, 16),), jnp.float32)
    dec_weight = normal_values(key_list[3], (LATENTS, D), (KB * 32) ** -0.5, 0.1875, ((0, 16),))
    dec_bias = normal_values(key_list[4], (D,), 0.5, 3.0, (), jnp.float32)
    active = different_ones(key_list[5], ROWBLOCKS, NBLK, KB, 2048)
    counts = draw_counts(jax.random.fold_in(key_list[7], 71), 0)
    return {"acts": acts, "enc_weight": enc_weight, "enc_bias": enc_bias, "dec_weight": dec_weight, "dec_bias": dec_bias, "active": active, "counts": counts}


def live_latents(active, counts):
    slots = jnp.arange(KB)[None, :] < counts[:, None]
    matches = (active[:, :, None] == jnp.arange(NBLK)[None, None, :]) & slots[:, :, None]
    blocks = jnp.any(matches, axis=1)
    return jnp.repeat(blocks, BLOCK, axis=1)


def reference(acts, enc_weight, enc_bias, dec_weight, dec_bias, active, counts):
    live = live_latents(active, counts)
    group_acts = acts.reshape(N_GROUP, GROUP_ROWS, D)
    group_live = live.reshape(N_GROUP, N_INDEX, LATENTS)
    dec_shards = dec_weight.reshape(N_INDEX, LAT_DEV, D)

    def one_group(carry, inputs):
        rows, mask = inputs
        preact = jnp.dot(rows, enc_weight, preferred_element_type=jnp.float32) + enc_bias
        row_mask = jnp.repeat(mask, TOK_DEV, axis=0)
        codes = jnp.where(row_mask, jnp.maximum(preact, 0.0), 0.0).astype(jnp.bfloat16)
        code_shards = codes.reshape(GROUP_ROWS, N_INDEX, LAT_DEV).transpose(1, 0, 2)

        def add_shard(total, pair):
            code_part, dec_part = pair
            part = jnp.dot(code_part, dec_part, preferred_element_type=jnp.float32).astype(jnp.bfloat16)
            part = lax.optimization_barrier(part)
            return total + part.astype(jnp.float32), None

        summed, _ = lax.scan(add_shard, jnp.zeros((GROUP_ROWS, D), jnp.float32), (code_shards, dec_shards))
        recon = (summed + dec_bias).astype(jnp.bfloat16)
        error = (recon.astype(jnp.float32) - rows.astype(jnp.float32)).astype(jnp.bfloat16)
        grad = jnp.dot(codes.T, error, preferred_element_type=jnp.float32).astype(jnp.bfloat16)
        grad = lax.optimization_barrier(grad)
        return carry + grad.astype(jnp.float32), recon

    dec_grad, recons = lax.scan(one_group, jnp.zeros((LATENTS, D), jnp.float32), (group_acts, group_live))
    return recons.reshape(TOKENS, D), dec_grad
```

```python
import jax
import jax.numpy as jnp
from jax import lax
from jax.sharding import PartitionSpec as P

BLOCK = 64
SIDE = 4
AXES = ("group", "index")
F32 = jnp.float32
BF16 = jnp.bfloat16


def device_of(y, core, z, x):
    return ((y * 2 + core) * SIDE + z) * SIDE + x


def ring_pairs(axis):
    pairs = []
    for y in range(SIDE):
        for core in range(2):
            for z in range(SIDE):
                for x in range(SIDE):
                    at = {"y": y, "z": z, "x": x}
                    to = dict(at)
                    to[axis] = (at[axis] + (1 if core == 0 else -1)) % SIDE
                    pairs.append(
                        (device_of(y, core, z, x), device_of(to["y"], core, to["z"], to["x"]))
                    )
    return pairs


RINGS = {axis: ring_pairs(axis) for axis in ("x", "y", "z")}
SWAP = [
    (device_of(y, core, z, x), device_of(y, 1 - core, z, x))
    for y in range(SIDE)
    for core in range(2)
    for z in range(SIDE)
    for x in range(SIDE)
]


def hop(block, axis):
    return lax.ppermute(block, AXES, RINGS[axis])


def ring_gather(block, axis):
    blocks = {0: block}
    for o in (3, 2, 1):
        block = hop(block, axis)
        blocks[o] = block
    return [blocks[o] for o in range(SIDE)]


def ring_reduce(parts, axis):
    total = parts[3]
    for o in (2, 1, 0):
        total = (hop(total, axis).astype(F32) + parts[o].astype(F32)).astype(BF16)
    return total


def body(acts, enc_weight, enc_bias, dec_weight, dec_bias, active, counts):
    tok_dev, width = acts.shape
    lat_dev = dec_weight.shape[0]
    half = tok_dev // 2
    chunks = 2
    cols = width // chunks
    my_index = lax.axis_index("index")
    my_group = lax.axis_index("group")
    core = my_group % 2
    my_y = my_group // 2
    my_z = my_index // SIDE
    my_x = my_index % SIDE
    ahead = jnp.where(core == 0, 1, SIDE - 1)

    own_count = lat_dev // BLOCK
    own_blocks = my_index * own_count + jnp.arange(own_count)
    slots = jnp.arange(active.shape[1])[None, :] < counts[:, None]
    matches = (active[:, :, None] == own_blocks[None, None, :]) & slots[:, :, None]
    block_live = jnp.any(matches, axis=1).astype(F32)

    orders = (("x", "z"), ("z", "x"))

    def live_rows(o2):
        o1 = jnp.arange(SIDE)
        steps_a = ((my_z + ahead * o2) % SIDE) * SIDE + (my_x + ahead * o1) % SIDE
        steps_b = ((my_z + ahead * o1) % SIDE) * SIDE + (my_x + ahead * o2) % SIDE
        live = block_live[jnp.concatenate([steps_a, steps_b])]
        return jnp.repeat(jnp.repeat(live, BLOCK, axis=1), half, axis=0)

    def gather(block, order):
        near = jnp.concatenate(ring_gather(block, order[0]), axis=0)
        return ring_gather(near, order[1])

    rows = [
        [gather(acts[h * half : (h + 1) * half, c * cols : (c + 1) * cols], orders[h]) for c in range(chunks)]
        for h in range(2)
    ]
    codes = {}
    for o2 in (0, 3, 2, 1):
        block = jnp.concatenate(
            [jnp.concatenate([rows[h][c][o2] for c in range(chunks)], axis=1) for h in range(2)], axis=0
        )
        preact = jnp.dot(block, enc_weight, preferred_element_type=F32) + enc_bias
        codes[o2] = jnp.where(live_rows(o2) > 0.0, jnp.maximum(preact, 0.0), 0.0).astype(BF16)

    codes_all = jnp.concatenate([codes[o2] for o2 in range(SIDE)], axis=0)
    part = lat_dev // 8
    picked = []
    for other in (0, 1):
        toward = ahead if other == 0 else SIDE - ahead
        for oy in range(SIDE):
            at = ((my_y + toward * oy) % SIDE) * 2 + (core + other) % 2
            picked.append(lax.dynamic_slice_in_dim(codes_all, at * part, part, axis=1))
    codes_own = jnp.concatenate(picked[:SIDE], axis=1)
    codes_other = jnp.concatenate(picked[SIDE:], axis=1)

    recon = []
    grads = []
    for c in range(chunks):
        dec = dec_weight[:, c * cols : (c + 1) * cols]
        partial = {}
        for o2 in (3, 2, 1, 0):
            partial[o2] = jnp.dot(codes[o2], dec, preferred_element_type=F32).astype(BF16)
        recon_c = []
        errors = []
        for h in range(2):
            n = SIDE * half
            near = ring_reduce([partial[o2][h * n : (h + 1) * n] for o2 in range(SIDE)], orders[h][1])
            summed = ring_reduce([near[o * half : (o + 1) * half] for o in range(SIDE)], orders[h][0])
            mine = (summed.astype(F32) + dec_bias[c * cols : (c + 1) * cols]).astype(BF16)
            own = acts[h * half : (h + 1) * half, c * cols : (c + 1) * cols]
            error = (mine.astype(F32) - own.astype(F32)).astype(BF16)
            recon_c.append(mine)
            errors.append(gather(error, orders[h]))
        recon.append(jnp.concatenate(recon_c, axis=0))
        error_all = jnp.concatenate(
            [jnp.concatenate([errors[0][o2], errors[1][o2]], axis=0) for o2 in range(SIDE)], axis=0
        )

        def grad_of(codes_part):
            return lax.dot_general(
                codes_part, error_all, (((0,), (0,)), ((), ())), preferred_element_type=F32
            ).astype(BF16)

        theirs = lax.ppermute(grad_of(codes_other), AXES, SWAP)
        pair = grad_of(codes_own).astype(F32) + theirs.astype(F32)
        pair = pair.astype(BF16)
        grads.append(ring_reduce([pair[o * part : (o + 1) * part] for o in range(SIDE)], "y").astype(F32))
    return (jnp.concatenate(recon, axis=1), jnp.concatenate(grads, axis=1))


def solution(mesh):
    in_specs = (
        P(("group", "index"), None),
        P(None, "index"),
        P("index"),
        P("index", None),
        P(),
        P("group", None),
        P("group"),
    )
    out_specs = (P(("group", "index"), None), P(("index", "group"), None))
    return jax.shard_map(body, mesh=mesh, in_specs=in_specs, out_specs=out_specs, check_vma=False)
```

```python
import jax
import jax.numpy as jnp
from jax import lax
from jax.experimental import pallas as pl
from jax.experimental.pallas import tpu as pltpu
from jax.sharding import PartitionSpec as P

BLOCK = 64
SIDE = 4
CAP = 48
AXES = ("group", "index")
F32 = jnp.float32
BF16 = jnp.bfloat16
I32 = jnp.int32


def device_of(y, core, z, x):
    return ((y * 2 + core) * SIDE + z) * SIDE + x


def ring_pairs(axis):
    pairs = []
    for y in range(SIDE):
        for core in range(2):
            for z in range(SIDE):
                for x in range(SIDE):
                    at = {"y": y, "z": z, "x": x}
                    to = dict(at)
                    to[axis] = (at[axis] + (1 if core == 0 else -1)) % SIDE
                    pairs.append(
                        (device_of(y, core, z, x), device_of(to["y"], core, to["z"], to["x"]))
                    )
    return pairs


RINGS = {axis: ring_pairs(axis) for axis in ("x", "y", "z")}


def hop(block, axis):
    return lax.ppermute(block, AXES, RINGS[axis])


def ring_gather(block, axis):
    blocks = {0: block}
    for o in (3, 2, 1):
        block = hop(block, axis)
        blocks[o] = block
    return jnp.concatenate([blocks[o] for o in range(SIDE)], axis=0)


def pack_kernel(pair_ref, codes_ref, out_ref):
    left = lax.broadcasted_iota(I32, (BLOCK // 2, 2 * BLOCK), 1) < BLOCK

    def one(j, carry):
        pair = pair_ref[j]
        row = pl.multiple_of((pair // 16) * BLOCK, BLOCK)
        col = pl.multiple_of(((pair % 16) // 2) * (2 * BLOCK), 2 * BLOCK)
        tile = codes_ref[pl.ds(row, BLOCK), pl.ds(col, 2 * BLOCK)].astype(F32)
        turned = pltpu.roll(tile, BLOCK, 1)
        odd = pair % 2 == 1
        to_left = jnp.where(odd, turned, tile)
        to_right = jnp.where(odd, tile, turned)
        packed = jnp.where(left, to_left[: BLOCK // 2], to_right[BLOCK // 2 :])
        out_ref[pl.ds(pl.multiple_of(j * (BLOCK // 2), BLOCK // 2), BLOCK // 2), :] = packed.astype(BF16)
        return carry

    lax.fori_loop(0, CAP, one, 0)


def pack(pairs, codes):
    return pl.pallas_call(
        pack_kernel,
        out_shape=jax.ShapeDtypeStruct((CAP * BLOCK // 2, 2 * BLOCK), BF16),
        in_specs=[
            pl.BlockSpec(memory_space=pltpu.SMEM),
            pl.BlockSpec(memory_space=pltpu.VMEM),
        ],
        out_specs=pl.BlockSpec(memory_space=pltpu.VMEM),
        compiler_params=pltpu.CompilerParams(vmem_limit_bytes=16 * 2**20),
    )(pairs, codes)


def place(block):
    return pl.multiple_of((((block % 16) // 2) * 16 + block // 16) * (2 * BLOCK) + (block % 2) * BLOCK, BLOCK)


def slice_kernel(active_ref, slot_ref, counts_ref, packed_ref, dec_ref, acts_ref, bias_ref, recon_ref, grad_ref, lhs_ref, total_ref):
    half = BLOCK // 2
    cols = dec_ref.shape[1]
    rows = dec_ref.shape[0]
    left = lax.broadcasted_iota(I32, (half, 2 * BLOCK), 1) < BLOCK
    step = 512

    def clear(j, carry):
        total_ref[pl.ds(pl.multiple_of(j * step, step), step), :] = jnp.zeros((step, cols), F32)
        return carry

    lax.fori_loop(0, rows // step, clear, 0)

    def row_block(r, carry):
        count = counts_ref[r]
        quads = (count + 3) // 4

        def load(s):
            slot = slot_ref[r, s]
            tile = packed_ref[pl.ds(pl.multiple_of(slot * half, half), half), :].astype(F32)
            return jnp.where(s < count, tile, 0.0)

        def pair(s):
            first, second = load(s), load(s + 1)
            top = jnp.where(left, first, pltpu.roll(second, BLOCK, 1))
            bottom = jnp.where(left, pltpu.roll(first, BLOCK, 1), second)
            return jnp.concatenate([top, bottom], axis=0)

        def decode(q, total):
            s = q * 4
            lhs = jnp.concatenate([pair(s), pair(s + 2)], axis=1).astype(BF16)
            lhs_ref[q] = lhs
            dec = jnp.concatenate([dec_ref[pl.ds(place(active_ref[r, s + k]), BLOCK), :] for k in range(4)], axis=0)
            return total + jnp.dot(lhs, dec, preferred_element_type=F32)

        at = pl.ds(pl.multiple_of(r * BLOCK, BLOCK), BLOCK)
        total = lax.fori_loop(0, quads, decode, jnp.zeros((BLOCK, cols), F32))
        recon = (total + bias_ref[...]).astype(BF16)
        recon_ref[at, :] = recon
        error = (recon.astype(F32) - acts_ref[at, :].astype(F32)).astype(BF16)

        def gradient(q, carry):
            s = q * 4
            part = lax.dot_general(lhs_ref[q], error, (((0,), (0,)), ((), ())), preferred_element_type=F32)
            for k in range(4):
                to = pl.ds(place(active_ref[r, s + k]), BLOCK)
                total_ref[to, :] += part[k * BLOCK : (k + 1) * BLOCK]
            return carry

        lax.fori_loop(0, quads, gradient, 0)
        return carry

    lax.fori_loop(0, counts_ref.shape[0], row_block, 0)

    def narrow(j, carry):
        at = pl.ds(pl.multiple_of(j * step, step), step)
        grad_ref[at, :] = total_ref[at, :].astype(BF16)
        return carry

    lax.fori_loop(0, rows // step, narrow, 0)


def column_slice(active, slot, counts, packed, dec, acts, bias):
    rows, cols = dec.shape
    tokens = acts.shape[0]
    slots = active.shape[1]
    smem = pl.BlockSpec(memory_space=pltpu.SMEM)
    vmem = pl.BlockSpec(memory_space=pltpu.VMEM)
    return pl.pallas_call(
        slice_kernel,
        out_shape=(
            jax.ShapeDtypeStruct((tokens, cols), BF16),
            jax.ShapeDtypeStruct((rows, cols), BF16),
        ),
        in_specs=[smem, smem, smem, vmem, vmem, vmem, vmem],
        out_specs=(vmem, vmem),
        scratch_shapes=[
            pltpu.VMEM((slots // 4, BLOCK, 4 * BLOCK), BF16),
            pltpu.VMEM((rows, cols), F32),
        ],
        compiler_params=pltpu.CompilerParams(vmem_limit_bytes=56 * 2**20),
    )(active, slot, counts, packed, dec, acts, bias)


def body(acts, enc_weight, enc_bias, dec_weight, dec_bias, active, counts):
    tok_dev, width = acts.shape
    lat_dev = dec_weight.shape[0]
    n_index = lax.axis_size("index")
    n_group = lax.axis_size("group")
    cols = width // n_index
    part = lat_dev // n_group
    own_count = lat_dev // BLOCK
    n_blocks = own_count * n_index
    my_index = lax.axis_index("index")
    my_group = lax.axis_index("group")
    my_z, my_x = my_index // SIDE, my_index % SIDE
    ahead = jnp.where(my_group % 2 == 0, 1, SIDE - 1)

    rows = lax.all_gather(acts, "index", axis=0, tiled=True)

    mine = lax.dynamic_slice_in_dim(dec_weight, my_group * part, part, axis=0)
    mine = mine.reshape(part, n_index, cols).transpose(1, 0, 2)
    mine = lax.all_to_all(mine, "index", 0, 0, tiled=True)
    dec_cols = lax.all_gather(mine.reshape(n_index * part, cols), "group", axis=0, tiled=True)

    slots = jnp.arange(active.shape[1])[None, :] < counts[:, None]
    is_block = active[:, :, None] == jnp.arange(n_blocks)[None, None, :]
    live = jnp.any(is_block & slots[:, :, None], axis=1)
    by_owner = live.reshape(n_index, n_index, own_count).transpose(1, 0, 2).reshape(n_index, n_index * own_count)
    pair_at = jnp.arange(n_index * own_count)
    upto = (pair_at[:, None] <= pair_at[None, :]).astype(BF16)
    ranks = jnp.dot(by_owner.astype(BF16), upto, preferred_element_type=F32).astype(I32)
    most = jnp.max(ranks[:, -1])
    most = lax.pmax(most, "group")
    ranks = jnp.where(by_owner, ranks - 1, -1)

    own_ranks = lax.dynamic_index_in_dim(ranks, my_index, 0, keepdims=False)
    pairs = jnp.sum(
        jnp.where(own_ranks[None, :] == jnp.arange(CAP)[:, None], pair_at[None, :], 0), axis=1
    ).astype(I32)

    owner = jnp.arange(n_index)
    dz = (ahead * (owner // SIDE - my_z + SIDE)) % SIDE
    dx = (ahead * (owner % SIDE - my_x + SIDE)) % SIDE
    half = CAP // 2
    first = ((dz * SIDE + dx) * half)[:, None] + ranks
    second = ((n_index + dx * SIDE + dz) * half)[:, None] + ranks - half
    table = jnp.where(ranks < half, first, second)
    table = table.reshape(n_index, n_index, own_count).transpose(1, 0, 2).reshape(n_index, n_blocks)
    slot = jnp.sum(jnp.where(is_block & slots[:, :, None], table[:, None, :], 0), axis=2).astype(I32)
    slot = jnp.clip(slot, 0, n_index * CAP - 1)

    preact = jnp.dot(rows, enc_weight, preferred_element_type=F32) + enc_bias
    codes_any = jnp.maximum(preact, 0.0).astype(BF16)

    def packed_path():
        packed = pack(pairs, codes_any)
        n = packed.shape[0] // 2
        one = ring_gather(ring_gather(packed[:n], "x"), "z")
        two = ring_gather(ring_gather(packed[n:], "z"), "x")
        packed = jnp.concatenate([one, two], axis=0)
        acts_cols = lax.dynamic_slice_in_dim(rows, my_index * cols, cols, axis=1)
        bias_cols = lax.dynamic_slice_in_dim(dec_bias, my_index * cols, cols, axis=0)[None, :]
        recon, grad = column_slice(active, slot, counts, packed, dec_cols, acts_cols, bias_cols)
        grad = lax.psum_scatter(grad, "group", scatter_dimension=0, tiled=True)
        recon = lax.all_to_all(recon.reshape(n_index, tok_dev, cols), "index", 0, 0, tiled=True)
        grad = lax.all_to_all(grad.reshape(n_index, part, cols), "index", 0, 0, tiled=True)
        recon = recon.transpose(1, 0, 2).reshape(tok_dev, width)
        grad = grad.transpose(1, 0, 2).reshape(part, width).astype(F32)
        return recon, grad

    def dense_path():
        own_live = lax.dynamic_slice_in_dim(live, my_index * own_count, own_count, axis=1)
        row_live = jnp.repeat(jnp.repeat(own_live, BLOCK, axis=1), tok_dev, axis=0)
        codes = jnp.where(row_live, codes_any, jnp.zeros((), BF16))
        summed = lax.psum_scatter(
            jnp.dot(codes, dec_weight, preferred_element_type=F32).astype(BF16),
            "index",
            scatter_dimension=0,
            tiled=True,
        ).astype(F32)
        recon = (summed + dec_bias).astype(BF16)
        error = (recon.astype(F32) - acts.astype(F32)).astype(BF16)
        error_all = lax.all_gather(error, "index", axis=0, tiled=True)
        grad = lax.dot_general(codes, error_all, (((0,), (0,)), ((), ())), preferred_element_type=F32)
        grad = lax.psum_scatter(grad.astype(BF16), "group", scatter_dimension=0, tiled=True)
        return recon, grad.astype(F32)

    return lax.cond(most <= CAP, packed_path, dense_path)


def solution(mesh):
    in_specs = (
        P(("group", "index"), None),
        P(None, "index"),
        P("index"),
        P("index", None),
        P(),
        P("group", None),
        P("group"),
    )
    out_specs = (P(("group", "index"), None), P(("index", "group"), None))
    return jax.shard_map(body, mesh=mesh, in_specs=in_specs, out_specs=out_specs, check_vma=False)
```

```python
import jax
import jax.numpy as jnp
from jax import lax
from jax.experimental import pallas as pl
from jax.experimental.pallas import tpu as pltpu
from jax.sharding import PartitionSpec as P

BLOCK = 64
SIDE = 4
CAP = 48
EIGHT = 8
AXES = ("group", "index")
F32 = jnp.float32
BF16 = jnp.bfloat16
I32 = jnp.int32


def device_of(y, core, z, x):
    return ((y * 2 + core) * SIDE + z) * SIDE + x


def ring_pairs(axis):
    pairs = []
    for y in range(SIDE):
        for core in range(2):
            for z in range(SIDE):
                for x in range(SIDE):
                    at = {"y": y, "z": z, "x": x}
                    to = dict(at)
                    to[axis] = (at[axis] + (1 if core == 0 else -1)) % SIDE
                    pairs.append(
                        (device_of(y, core, z, x), device_of(to["y"], core, to["z"], to["x"]))
                    )
    return pairs


RINGS = {axis: ring_pairs(axis) for axis in ("x", "y", "z")}


def hop(block, axis):
    return lax.ppermute(block, AXES, RINGS[axis])


def ring_gather(blocks, axes):
    slots = [{0: block} for block in blocks]
    for o in (3, 2, 1):
        blocks = lax.optimization_barrier([hop(block, axis) for block, axis in zip(blocks, axes)])
        for slot, block in zip(slots, blocks):
            slot[o] = block
    return [[slot[o] for o in range(SIDE)] for slot in slots]


def pack_kernel(pair_ref, codes_ref, out_ref):
    left = lax.broadcasted_iota(I32, (BLOCK // 2, 2 * BLOCK), 1) < BLOCK

    def one(j, carry):
        pair = pair_ref[j]
        row = pl.multiple_of((pair // 16) * BLOCK, BLOCK)
        col = pl.multiple_of(((pair % 16) // 2) * (2 * BLOCK), 2 * BLOCK)
        tile = codes_ref[pl.ds(row, BLOCK), pl.ds(col, 2 * BLOCK)].astype(F32)
        turned = pltpu.roll(tile, BLOCK, 1)
        odd = pair % 2 == 1
        to_left = jnp.where(odd, turned, tile)
        to_right = jnp.where(odd, tile, turned)
        packed = jnp.where(left, to_left[: BLOCK // 2], to_right[BLOCK // 2 :])
        out_ref[pl.ds(pl.multiple_of(j * (BLOCK // 2), BLOCK // 2), BLOCK // 2), :] = packed.astype(BF16)
        return carry

    lax.fori_loop(0, CAP, one, 0)


def pack(pairs, codes):
    return pl.pallas_call(
        pack_kernel,
        out_shape=jax.ShapeDtypeStruct((CAP * BLOCK // 2, 2 * BLOCK), BF16),
        in_specs=[
            pl.BlockSpec(memory_space=pltpu.SMEM),
            pl.BlockSpec(memory_space=pltpu.VMEM),
        ],
        out_specs=pl.BlockSpec(memory_space=pltpu.VMEM),
        compiler_params=pltpu.CompilerParams(vmem_limit_bytes=16 * 2**20),
    )(pairs, codes)


def place(block):
    return pl.multiple_of((((block % 16) // 2) * 16 + block // 16) * (2 * BLOCK) + (block % 2) * BLOCK, BLOCK)


def slice_kernel(active_ref, slot_ref, counts_ref, acts_ref, bias_ref, dec_hbm, *refs):
    pieces = refs[: 2 * SIDE]
    recon_ref, grad_ref, packed_ref, dec_ref, lhs_ref, total_ref, sems = refs[2 * SIDE :]
    half = BLOCK // 2
    rows, cols = dec_ref.shape
    size = pieces[0].shape[0]
    left = lax.broadcasted_iota(I32, (half, 2 * BLOCK), 1) < BLOCK
    step = 512

    copies = [pltpu.make_async_copy(dec_hbm, dec_ref, sems.at[2 * SIDE])]
    for k, piece in enumerate(pieces):
        copies.append(pltpu.make_async_copy(piece, packed_ref.at[pl.ds(k * size, size), :], sems.at[k]))
    for copy in copies:
        copy.start()

    def clear(j, carry):
        total_ref[pl.ds(pl.multiple_of(j * step, step), step), :] = jnp.zeros((step, cols), F32)
        return carry

    lax.fori_loop(0, rows // step, clear, 0)
    for copy in copies:
        copy.wait()

    def row_block(r, carry):
        count = counts_ref[r]
        steps = (count + EIGHT - 1) // EIGHT

        def load(s):
            slot = slot_ref[r, s]
            tile = packed_ref[pl.ds(pl.multiple_of(slot * half, half), half), :].astype(F32)
            return jnp.where(s < count, tile, 0.0)

        def pair(s):
            first, second = load(s), load(s + 1)
            top = jnp.where(left, first, pltpu.roll(second, BLOCK, 1))
            bottom = jnp.where(left, pltpu.roll(first, BLOCK, 1), second)
            return jnp.concatenate([top, bottom], axis=0)

        def decode(q, total):
            s = q * EIGHT
            lhs = jnp.concatenate([pair(s + k) for k in range(0, EIGHT, 2)], axis=1).astype(BF16)
            lhs_ref[q] = lhs
            dec = jnp.concatenate(
                [dec_ref[pl.ds(place(active_ref[r, s + k]), BLOCK), :] for k in range(EIGHT)], axis=0
            )
            return total + jnp.dot(lhs, dec, preferred_element_type=F32)

        at = pl.ds(pl.multiple_of(r * BLOCK, BLOCK), BLOCK)
        total = lax.fori_loop(0, steps, decode, jnp.zeros((BLOCK, cols), F32))
        recon = (total + bias_ref[...]).astype(BF16)
        recon_ref[at, :] = recon
        error = (recon.astype(F32) - acts_ref[at, :].astype(F32)).astype(BF16)

        def gradient(q, carry):
            s = q * EIGHT
            part = lax.dot_general(lhs_ref[q], error, (((0,), (0,)), ((), ())), preferred_element_type=F32)
            for k in range(EIGHT):
                to = pl.ds(place(active_ref[r, s + k]), BLOCK)
                total_ref[to, :] += part[k * BLOCK : (k + 1) * BLOCK]
            return carry

        lax.fori_loop(0, steps, gradient, 0)
        return carry

    lax.fori_loop(0, counts_ref.shape[0], row_block, 0)

    def narrow(j, carry):
        at = pl.ds(pl.multiple_of(j * step, step), step)
        grad_ref[at, :] = total_ref[at, :].astype(BF16)
        return carry

    lax.fori_loop(0, rows // step, narrow, 0)


def column_slice(active, slot, counts, pieces, dec, acts, bias):
    rows, cols = dec.shape
    tokens = acts.shape[0]
    slots = active.shape[1]
    smem = pl.BlockSpec(memory_space=pltpu.SMEM)
    vmem = pl.BlockSpec(memory_space=pltpu.VMEM)
    anywhere = pl.BlockSpec(memory_space=pl.ANY)
    return pl.pallas_call(
        slice_kernel,
        out_shape=(
            jax.ShapeDtypeStruct((tokens, cols), BF16),
            jax.ShapeDtypeStruct((rows, cols), BF16),
        ),
        in_specs=[smem, smem, smem, vmem, vmem] + [anywhere] * (1 + len(pieces)),
        out_specs=(vmem, vmem),
        scratch_shapes=[
            pltpu.VMEM((len(pieces) * pieces[0].shape[0], 2 * BLOCK), BF16),
            pltpu.VMEM((rows, cols), BF16),
            pltpu.VMEM((slots // EIGHT, BLOCK, EIGHT * BLOCK), BF16),
            pltpu.VMEM((rows, cols), F32),
            pltpu.SemaphoreType.DMA((len(pieces) + 1,)),
        ],
        compiler_params=pltpu.CompilerParams(vmem_limit_bytes=52 * 2**20),
    )(active, slot, counts, acts, bias, dec, *pieces)


def body(acts, enc_weight, enc_bias, dec_weight, dec_bias, active, counts):
    tok_dev, width = acts.shape
    lat_dev = dec_weight.shape[0]
    n_index = lax.axis_size("index")
    n_group = lax.axis_size("group")
    cols = width // n_index
    part = lat_dev // n_group
    own_count = lat_dev // BLOCK
    n_blocks = own_count * n_index
    my_index = lax.axis_index("index")
    my_group = lax.axis_index("group")
    my_z, my_x = my_index // SIDE, my_index % SIDE
    ahead = jnp.where(my_group % 2 == 0, 1, SIDE - 1)

    rows = lax.all_gather(acts, "index", axis=0, tiled=True)

    mine = lax.dynamic_slice_in_dim(dec_weight, my_group * part, part, axis=0)
    mine = mine.reshape(part, n_index, cols).transpose(1, 0, 2)
    mine = lax.all_to_all(mine, "index", 0, 0, tiled=True)

    slots = jnp.arange(active.shape[1])[None, :] < counts[:, None]
    is_block = active[:, :, None] == jnp.arange(n_blocks)[None, None, :]
    live = jnp.any(is_block & slots[:, :, None], axis=1)
    by_owner = live.reshape(n_index, n_index, own_count).transpose(1, 0, 2).reshape(n_index, n_index * own_count)
    pair_at = jnp.arange(n_index * own_count)
    upto = (pair_at[:, None] <= pair_at[None, :]).astype(BF16)
    ranks = jnp.dot(by_owner.astype(BF16), upto, preferred_element_type=F32).astype(I32)
    most = jnp.max(ranks[:, -1])
    most = lax.pmax(most, "group")
    ranks = jnp.where(by_owner, ranks - 1, -1)

    own_ranks = lax.dynamic_index_in_dim(ranks, my_index, 0, keepdims=False)
    pairs = jnp.sum(
        jnp.where(own_ranks[None, :] == jnp.arange(CAP)[:, None], pair_at[None, :], 0), axis=1
    ).astype(I32)

    owner = jnp.arange(n_index)
    dz = (ahead * (owner // SIDE - my_z + SIDE)) % SIDE
    dx = (ahead * (owner % SIDE - my_x + SIDE)) % SIDE
    half = CAP // 2
    first = ((dz * SIDE + dx) * half)[:, None] + ranks
    second = ((n_index + dx * SIDE + dz) * half)[:, None] + ranks - half
    table = jnp.where(ranks < half, first, second)
    table = table.reshape(n_index, n_index, own_count).transpose(1, 0, 2).reshape(n_index, n_blocks)
    slot = jnp.sum(jnp.where(is_block & slots[:, :, None], table[:, None, :], 0), axis=2).astype(I32)
    slot = jnp.clip(slot, 0, n_index * CAP - 1)

    preact = jnp.dot(rows, enc_weight, preferred_element_type=F32) + enc_bias
    codes_any = jnp.maximum(preact, 0.0).astype(BF16)

    def packed_path():
        dec_cols = lax.all_gather(mine.reshape(n_index * part, cols), "group", axis=0, tiled=True)
        packed = pack(pairs, codes_any)
        n = packed.shape[0] // 2
        near = [jnp.concatenate(parts, axis=0) for parts in ring_gather([packed[:n], packed[n:]], ("x", "z"))]
        one, two = ring_gather(near, ("z", "x"))
        acts_cols = lax.dynamic_slice_in_dim(rows, my_index * cols, cols, axis=1)
        bias_cols = lax.dynamic_slice_in_dim(dec_bias, my_index * cols, cols, axis=0)[None, :]
        recon, grad = column_slice(active, slot, counts, one + two, dec_cols, acts_cols, bias_cols)
        grad = lax.psum_scatter(grad, "group", scatter_dimension=0, tiled=True)
        recon = lax.all_to_all(recon.reshape(n_index, tok_dev, cols), "index", 0, 0, tiled=True)
        grad = lax.all_to_all(grad.reshape(n_index, part, cols), "index", 0, 0, tiled=True)
        recon = recon.transpose(1, 0, 2).reshape(tok_dev, width)
        grad = grad.transpose(1, 0, 2).reshape(part, width).astype(F32)
        return recon, grad

    def dense_path():
        own_live = lax.dynamic_slice_in_dim(live, my_index * own_count, own_count, axis=1)
        row_live = jnp.repeat(jnp.repeat(own_live, BLOCK, axis=1), tok_dev, axis=0)
        codes = jnp.where(row_live, codes_any, jnp.zeros((), BF16))
        summed = lax.psum_scatter(
            jnp.dot(codes, dec_weight, preferred_element_type=F32).astype(BF16),
            "index",
            scatter_dimension=0,
            tiled=True,
        ).astype(F32)
        recon = (summed + dec_bias).astype(BF16)
        error = (recon.astype(F32) - acts.astype(F32)).astype(BF16)
        error_all = lax.all_gather(error, "index", axis=0, tiled=True)
        grad = lax.dot_general(codes, error_all, (((0,), (0,)), ((), ())), preferred_element_type=F32)
        grad = lax.psum_scatter(grad.astype(BF16), "group", scatter_dimension=0, tiled=True)
        return recon, grad.astype(F32)

    return lax.cond(most <= CAP, packed_path, dense_path)


def solution(mesh):
    in_specs = (
        P(("group", "index"), None),
        P(None, "index"),
        P("index"),
        P("index", None),
        P(),
        P("group", None),
        P("group"),
    )
    out_specs = (P(("group", "index"), None), P(("index", "group"), None))
    return jax.shard_map(body, mesh=mesh, in_specs=in_specs, out_specs=out_specs, check_vma=False)
```

```python
import jax
import jax.numpy as jnp
from jax import lax
from jax.sharding import PartitionSpec as P

BLOCK = 64
SIDE = 4
TRAINS = 1
TAIL = 4
DIRECT = (2, 1, 3)
AXES = ("group", "index")
F32 = jnp.float32
BF16 = jnp.bfloat16


def device_of(y, core, z, x):
    return ((y * 2 + core) * SIDE + z) * SIDE + x


def shift_pairs(axis, by):
    pairs = []
    for y in range(SIDE):
        for core in range(2):
            for z in range(SIDE):
                for x in range(SIDE):
                    to = {"y": y, "z": z, "x": x}
                    to[axis] = (to[axis] + (by if core == 0 else -by)) % SIDE
                    pairs.append(
                        (device_of(y, core, z, x), device_of(to["y"], core, to["z"], to["x"]))
                    )
    return pairs


SHIFTS = {(axis, by): shift_pairs(axis, by) for axis in ("x", "y", "z") for by in (1, 2, 3)}
SWAP = [
    (device_of(y, core, z, x), device_of(y, 1 - core, z, x))
    for y in range(SIDE)
    for core in range(2)
    for z in range(SIDE)
    for x in range(SIDE)
]
ARRIVAL = (0, 3, 2, 1)


def shift(block, axis, by):
    return lax.ppermute(block, AXES, SHIFTS[axis, by])


def together(blocks):
    return lax.optimization_barrier(blocks)


def after(blocks, earlier):
    return lax.optimization_barrier((blocks, earlier))[0]


def direct_gather(block, axis):
    slot = {0: block}
    for o in DIRECT:
        slot[o] = shift(block, axis, SIDE - o)
    return [slot[o] for o in range(SIDE)]


def direct_reduce(parts, axis):
    arrived = [shift(parts[o], axis, o) for o in DIRECT]
    total = parts[0].astype(F32)
    for block in arrived:
        total = total + block.astype(F32)
    return total


def near_gather(blocks, axes, direct):
    if direct:
        return [direct_gather(block, axis) for block, axis in zip(blocks, axes)]
    slots = [{0: block} for block in blocks]
    for o in (3, 2, 1):
        blocks = together([shift(block, axis, 1) for block, axis in zip(blocks, axes)])
        for slot, block in zip(slots, blocks):
            slot[o] = block
    return [[slot[o] for o in range(SIDE)] for slot in slots]


def near_reduce(parts, axes, direct):
    if direct:
        return [direct_reduce(part, axis) for part, axis in zip(parts, axes)]
    totals = [part[3] for part in parts]
    for o in (2, 1, 0):
        totals = together([shift(total, axis, 1) for total, axis in zip(totals, axes)])
        totals = [total.astype(F32) + part[o].astype(F32) for total, part in zip(totals, parts)]
        if o > 0:
            totals = [total.astype(BF16) for total in totals]
    return totals


def rings(first, following, axes):
    n = len(first)
    ready = [first[t] for t in range(n)]
    landed = {}
    for k, o in enumerate((3, 2, 1)):
        for t in range(n):
            blocks = ready[t]
            if t > 0 and k > 0:
                blocks = after(blocks, landed[t - 1, k - 1])
            if t == 0 and k > 1 and n > 1:
                blocks = after(blocks, landed[n - 1, k - 2])
            landed[t, k] = together([shift(block, axis, 1) for block, axis in zip(blocks, axes)])
        for t in range(n):
            ready[t] = following(t, o, landed[t, k])
    return ready


def body(acts, enc_weight, enc_bias, dec_weight, dec_bias, active, counts):
    tok_dev, width = acts.shape
    lat_dev = dec_weight.shape[0]
    half = tok_dev // 2
    my_index = lax.axis_index("index")
    my_group = lax.axis_index("group")
    core = my_group % 2
    my_y = my_group // 2
    my_z = my_index // SIDE
    my_x = my_index % SIDE
    ahead = jnp.where(core == 0, 1, SIDE - 1)

    own_count = lat_dev // BLOCK
    own_blocks = my_index * own_count + jnp.arange(own_count)
    slots = jnp.arange(active.shape[1])[None, :] < counts[:, None]
    matches = (active[:, :, None] == own_blocks[None, None, :]) & slots[:, :, None]
    block_live = jnp.any(matches, axis=1).astype(F32)

    def live_rows(o2):
        o1 = jnp.arange(SIDE)
        steps_a = ((my_z + ahead * o2) % SIDE) * SIDE + (my_x + ahead * o1) % SIDE
        steps_b = ((my_z + ahead * o1) % SIDE) * SIDE + (my_x + ahead * o2) % SIDE
        live = block_live[jnp.concatenate([steps_a, steps_b])]
        return jnp.repeat(jnp.repeat(live, BLOCK, axis=1), half, axis=0)

    near_axes, far_axes = ("x", "z"), ("z", "x")
    span = SIDE // TRAINS

    def gather(blocks, direct):
        near = near_gather(blocks, near_axes, direct)
        first = [
            [jnp.concatenate(near[h][t * span : (t + 1) * span], axis=0) for h in range(2)] for t in range(TRAINS)
        ]
        pieces = {(0, t): first[t] for t in range(TRAINS)}

        def keep(t, o, landed):
            pieces[o, t] = landed
            return landed

        rings(first, keep, far_axes)
        return [[pieces[o, t][h] for h in range(2) for t in range(TRAINS)] for o in range(SIDE)]

    halves = [acts[:half], acts[half:]]
    rows = gather(halves, False)
    codes = {}
    for o2 in ARRIVAL:
        preact = jnp.dot(jnp.concatenate(rows[o2], axis=0), enc_weight, preferred_element_type=F32) + enc_bias
        codes[o2] = jnp.where(live_rows(o2) > 0.0, jnp.maximum(preact, 0.0), 0.0).astype(BF16)

    codes_all = jnp.concatenate([codes[o2] for o2 in ARRIVAL], axis=0)
    part = lat_dev // 8
    picked = []
    for other in (0, 1):
        toward = ahead if other == 0 else SIDE - ahead
        for oy in range(SIDE):
            at = ((my_y + toward * oy) % SIDE) * 2 + (core + other) % 2
            picked.append(lax.dynamic_slice_in_dim(codes_all, at * part, part, axis=1))
    codes_own = jnp.concatenate(picked[:SIDE], axis=1)
    codes_other = jnp.concatenate(picked[SIDE:], axis=1)

    partial = {}
    for o2 in (3, 2, 1, 0):
        partial[o2] = jnp.dot(codes[o2], dec_weight, preferred_element_type=F32).astype(BF16)
    n = half * span

    def own_part(t, o):
        return [partial[o][(h * TRAINS + t) * n : (h * TRAINS + t + 1) * n] for h in range(2)]

    def add_own(t, o, landed):
        return [
            (block.astype(F32) + own.astype(F32)).astype(BF16) for block, own in zip(landed, own_part(t, o - 1))
        ]

    sums = rings([own_part(t, 3) for t in range(TRAINS)], add_own, far_axes)
    parts = [
        [sums[t][h][i * half : (i + 1) * half] for t in range(TRAINS) for i in range(span)] for h in range(2)
    ]
    recons = [(total + dec_bias).astype(BF16) for total in near_reduce(parts, near_axes, True)]
    errors = gather(
        [(recon.astype(F32) - own.astype(F32)).astype(BF16) for recon, own in zip(recons, halves)],
        False,
    )
    error_all = jnp.concatenate([block for o2 in ARRIVAL for block in errors[o2]], axis=0)

    cols = width // TAIL
    pairs = []
    for c in range(TAIL):

        def grad_of(codes_part):
            return lax.dot_general(
                codes_part,
                error_all[:, c * cols : (c + 1) * cols],
                (((0,), (0,)), ((), ())),
                preferred_element_type=F32,
            ).astype(BF16)

        theirs = lax.ppermute(grad_of(codes_other), AXES, SWAP)
        pair = (grad_of(codes_own).astype(F32) + theirs.astype(F32)).astype(BF16)
        pairs.append([pair[o * part : (o + 1) * part] for o in range(SIDE)])

    def add_pair(t, o, landed):
        total = landed[0].astype(F32) + pairs[t][o - 1].astype(F32)
        return [total.astype(BF16)]

    grads = rings([[pair[3]] for pair in pairs], add_pair, ("y",))
    grads = [total[0].astype(F32) for total in grads]
    return jnp.concatenate(recons, axis=0), jnp.concatenate(grads, axis=1)


def solution(mesh):
    in_specs = (
        P(("group", "index"), None),
        P(None, "index"),
        P("index"),
        P("index", None),
        P(),
        P("group", None),
        P("group"),
    )
    out_specs = (P(("group", "index"), None), P(("index", "group"), None))
    return jax.shard_map(body, mesh=mesh, in_specs=in_specs, out_specs=out_specs, check_vma=False)
```

```python
import jax
import jax.numpy as jnp
from jax import lax
from jax.sharding import PartitionSpec as P

BLOCK = 64
SIDE = 4
TRAINS = 1
TAIL = 4
DIRECT = (2, 1, 3)
FIRST, LAST = (1, 3), 2
AXES = ("group", "index")
F32 = jnp.float32
BF16 = jnp.bfloat16


def device_of(y, core, z, x):
    return ((y * 2 + core) * SIDE + z) * SIDE + x


def shift_pairs(axis, by):
    pairs = []
    for y in range(SIDE):
        for core in range(2):
            for z in range(SIDE):
                for x in range(SIDE):
                    to = {"y": y, "z": z, "x": x}
                    to[axis] = (to[axis] + (by if core == 0 else -by)) % SIDE
                    pairs.append(
                        (device_of(y, core, z, x), device_of(to["y"], core, to["z"], to["x"]))
                    )
    return pairs


SHIFTS = {(axis, by): shift_pairs(axis, by) for axis in ("x", "y", "z") for by in (1, 2, 3)}
SWAP = [
    (device_of(y, core, z, x), device_of(y, 1 - core, z, x))
    for y in range(SIDE)
    for core in range(2)
    for z in range(SIDE)
    for x in range(SIDE)
]
ARRIVAL = (0, 3, 2, 1)


def shift(block, axis, by):
    return lax.ppermute(block, AXES, SHIFTS[axis, by])


def together(blocks):
    return lax.optimization_barrier(blocks)


def after(blocks, earlier):
    return lax.optimization_barrier((blocks, earlier))[0]


def direct_gather(block, axis):
    slot = {0: block}
    for o in DIRECT:
        slot[o] = shift(block, axis, SIDE - o)
    return [slot[o] for o in range(SIDE)]


def direct_reduce(parts, axis):
    arrived = [shift(parts[o], axis, o) for o in DIRECT]
    total = parts[0].astype(F32)
    for block in arrived:
        total = total + block.astype(F32)
    return total


def near_gather(blocks, axes, direct):
    if direct:
        sides = together([shift(block, axis, by) for block, axis in zip(blocks, axes) for by in FIRST])
        blocks_late = after(blocks, sides)
        far = together([shift(block, axis, LAST) for block, axis in zip(blocks_late, axes)])
        slots = []
        for h, block in enumerate(blocks):
            slot = {0: block, SIDE - LAST: far[h]}
            for k, by in enumerate(FIRST):
                slot[SIDE - by] = sides[2 * h + k]
            slots.append([slot[o] for o in range(SIDE)])
        return slots
    slots = [{0: block} for block in blocks]
    for o in (3, 2, 1):
        blocks = together([shift(block, axis, 1) for block, axis in zip(blocks, axes)])
        for slot, block in zip(slots, blocks):
            slot[o] = block
    return [[slot[o] for o in range(SIDE)] for slot in slots]


def near_reduce(parts, axes, direct):
    if direct:
        return [direct_reduce(part, axis) for part, axis in zip(parts, axes)]
    totals = [part[3] for part in parts]
    for o in (2, 1, 0):
        totals = together([shift(total, axis, 1) for total, axis in zip(totals, axes)])
        totals = [total.astype(F32) + part[o].astype(F32) for total, part in zip(totals, parts)]
        if o > 0:
            totals = [total.astype(BF16) for total in totals]
    return totals


def rings(first, following, axes):
    n = len(first)
    ready = [first[t] for t in range(n)]
    landed = {}
    for k, o in enumerate((3, 2, 1)):
        for t in range(n):
            blocks = ready[t]
            if t > 0 and k > 0:
                blocks = after(blocks, landed[t - 1, k - 1])
            if t == 0 and k > 1 and n > 1:
                blocks = after(blocks, landed[n - 1, k - 2])
            landed[t, k] = together([shift(block, axis, 1) for block, axis in zip(blocks, axes)])
        for t in range(n):
            ready[t] = following(t, o, landed[t, k])
    return ready


def body(acts, enc_weight, enc_bias, dec_weight, dec_bias, active, counts):
    tok_dev, width = acts.shape
    lat_dev = dec_weight.shape[0]
    half = tok_dev // 2
    my_index = lax.axis_index("index")
    my_group = lax.axis_index("group")
    core = my_group % 2
    my_y = my_group // 2
    my_z = my_index // SIDE
    my_x = my_index % SIDE
    ahead = jnp.where(core == 0, 1, SIDE - 1)

    own_count = lat_dev // BLOCK
    own_blocks = my_index * own_count + jnp.arange(own_count)
    slots = jnp.arange(active.shape[1])[None, :] < counts[:, None]
    matches = (active[:, :, None] == own_blocks[None, None, :]) & slots[:, :, None]
    block_live = jnp.any(matches, axis=1).astype(F32)

    def live_rows(o2):
        o1 = jnp.arange(SIDE)
        steps_a = ((my_z + ahead * o2) % SIDE) * SIDE + (my_x + ahead * o1) % SIDE
        steps_b = ((my_z + ahead * o1) % SIDE) * SIDE + (my_x + ahead * o2) % SIDE
        live = block_live[jnp.concatenate([steps_a, steps_b])]
        return jnp.repeat(jnp.repeat(live, BLOCK, axis=1), half, axis=0)

    near_axes, far_axes = ("x", "z"), ("z", "x")
    span = SIDE // TRAINS

    def gather(blocks, direct):
        near = near_gather(blocks, near_axes, direct)
        first = [
            [jnp.concatenate(near[h][t * span : (t + 1) * span], axis=0) for h in range(2)] for t in range(TRAINS)
        ]
        pieces = {(0, t): first[t] for t in range(TRAINS)}

        def keep(t, o, landed):
            pieces[o, t] = landed
            return landed

        rings(first, keep, far_axes)
        return [[pieces[o, t][h] for h in range(2) for t in range(TRAINS)] for o in range(SIDE)]

    halves = [acts[:half], acts[half:]]
    rows = gather(halves, False)
    codes = {}
    for o2 in ARRIVAL:
        preact = jnp.dot(jnp.concatenate(rows[o2], axis=0), enc_weight, preferred_element_type=F32) + enc_bias
        codes[o2] = jnp.where(live_rows(o2) > 0.0, jnp.maximum(preact, 0.0), 0.0).astype(BF16)

    codes_all = jnp.concatenate([codes[o2] for o2 in ARRIVAL], axis=0)
    part = lat_dev // 8
    picked = []
    for other in (0, 1):
        toward = ahead if other == 0 else SIDE - ahead
        for oy in range(SIDE):
            at = ((my_y + toward * oy) % SIDE) * 2 + (core + other) % 2
            picked.append(lax.dynamic_slice_in_dim(codes_all, at * part, part, axis=1))
    codes_own = jnp.concatenate(picked[:SIDE], axis=1)
    codes_other = jnp.concatenate(picked[SIDE:], axis=1)

    partial = {}
    for o2 in (3, 2, 1, 0):
        partial[o2] = jnp.dot(codes[o2], dec_weight, preferred_element_type=F32).astype(BF16)
    n = half * span

    def own_part(t, o):
        return [partial[o][(h * TRAINS + t) * n : (h * TRAINS + t + 1) * n] for h in range(2)]

    def add_own(t, o, landed):
        return [
            (block.astype(F32) + own.astype(F32)).astype(BF16) for block, own in zip(landed, own_part(t, o - 1))
        ]

    sums = rings([own_part(t, 3) for t in range(TRAINS)], add_own, far_axes)
    parts = [
        [sums[t][h][i * half : (i + 1) * half] for t in range(TRAINS) for i in range(span)] for h in range(2)
    ]
    recons = [(total + dec_bias).astype(BF16) for total in near_reduce(parts, near_axes, True)]
    errors = gather(
        [(recon.astype(F32) - own.astype(F32)).astype(BF16) for recon, own in zip(recons, halves)],
        True,
    )
    error_all = jnp.concatenate([block for o2 in ARRIVAL for block in errors[o2]], axis=0)

    cols = width // TAIL
    pairs = []
    for c in range(TAIL):

        def grad_of(codes_part):
            return lax.dot_general(
                codes_part,
                error_all[:, c * cols : (c + 1) * cols],
                (((0,), (0,)), ((), ())),
                preferred_element_type=F32,
            ).astype(BF16)

        theirs = lax.ppermute(grad_of(codes_other), AXES, SWAP)
        pair = (grad_of(codes_own).astype(F32) + theirs.astype(F32)).astype(BF16)
        pairs.append([pair[o * part : (o + 1) * part] for o in range(SIDE)])

    def add_pair(t, o, landed):
        total = landed[0].astype(F32) + pairs[t][o - 1].astype(F32)
        return [total.astype(BF16)]

    grads = rings([[pair[3]] for pair in pairs], add_pair, ("y",))
    grads = [total[0].astype(F32) for total in grads]
    return jnp.concatenate(recons, axis=0), jnp.concatenate(grads, axis=1)


def solution(mesh):
    in_specs = (
        P(("group", "index"), None),
        P(None, "index"),
        P("index"),
        P("index", None),
        P(),
        P("group", None),
        P("group"),
    )
    out_specs = (P(("group", "index"), None), P(("index", "group"), None))
    return jax.shard_map(body, mesh=mesh, in_specs=in_specs, out_specs=out_specs, check_vma=False)
```

```python
import jax
import jax.numpy as jnp
from jax import lax
from jax.sharding import PartitionSpec as P

BLOCK = 64
SIDE = 4
TRAINS = 1
TAIL = 4
DIRECT = (2, 1, 3)
FIRST, LAST = (1, 3), 2
AXES = ("group", "index")
F32 = jnp.float32
BF16 = jnp.bfloat16


def device_of(y, core, z, x):
    return ((y * 2 + core) * SIDE + z) * SIDE + x


def shift_pairs(axis, by):
    pairs = []
    for y in range(SIDE):
        for core in range(2):
            for z in range(SIDE):
                for x in range(SIDE):
                    to = {"y": y, "z": z, "x": x}
                    to[axis] = (to[axis] + (by if core == 0 else -by)) % SIDE
                    pairs.append(
                        (device_of(y, core, z, x), device_of(to["y"], core, to["z"], to["x"]))
                    )
    return pairs


SHIFTS = {(axis, by): shift_pairs(axis, by) for axis in ("x", "y", "z") for by in (1, 2, 3)}
SWAP = [
    (device_of(y, core, z, x), device_of(y, 1 - core, z, x))
    for y in range(SIDE)
    for core in range(2)
    for z in range(SIDE)
    for x in range(SIDE)
]
ARRIVAL = (0, 3, 2, 1)


def shift(block, axis, by):
    return lax.ppermute(block, AXES, SHIFTS[axis, by])


def together(blocks):
    return lax.optimization_barrier(blocks)


def after(blocks, earlier):
    return lax.optimization_barrier((blocks, earlier))[0]


def direct_gather(block, axis):
    slot = {0: block}
    for o in DIRECT:
        slot[o] = shift(block, axis, SIDE - o)
    return [slot[o] for o in range(SIDE)]


def direct_reduce(parts, axis):
    arrived = [shift(parts[o], axis, o) for o in DIRECT]
    total = parts[0].astype(F32)
    for block in arrived:
        total = total + block.astype(F32)
    return total


def near_gather(blocks, axes, direct):
    if direct:
        sides = together([shift(block, axis, by) for block, axis in zip(blocks, axes) for by in FIRST])
        blocks_late = after(blocks, sides)
        far = together([shift(block, axis, LAST) for block, axis in zip(blocks_late, axes)])
        slots = []
        for h, block in enumerate(blocks):
            slot = {0: block, SIDE - LAST: far[h]}
            for k, by in enumerate(FIRST):
                slot[SIDE - by] = sides[2 * h + k]
            slots.append([slot[o] for o in range(SIDE)])
        return slots
    slots = [{0: block} for block in blocks]
    for o in (3, 2, 1):
        blocks = together([shift(block, axis, 1) for block, axis in zip(blocks, axes)])
        for slot, block in zip(slots, blocks):
            slot[o] = block
    return [[slot[o] for o in range(SIDE)] for slot in slots]


def near_reduce(parts, axes, direct):
    if direct:
        return [direct_reduce(part, axis) for part, axis in zip(parts, axes)]
    totals = [part[3] for part in parts]
    for o in (2, 1, 0):
        totals = together([shift(total, axis, 1) for total, axis in zip(totals, axes)])
        totals = [total.astype(F32) + part[o].astype(F32) for total, part in zip(totals, parts)]
        if o > 0:
            totals = [total.astype(BF16) for total in totals]
    return totals


def rings(first, following, axes, in_step=True):
    n = len(first)
    ready = [first[t] for t in range(n)]
    landed = {}
    for k, o in enumerate((3, 2, 1)):
        for t in range(n):
            blocks = ready[t]
            if t > 0 and k > 0:
                blocks = after(blocks, landed[t - 1, k - 1])
            if t == 0 and k > 1 and n > 1:
                blocks = after(blocks, landed[n - 1, k - 2])
            hops = [shift(block, axis, 1) for block, axis in zip(blocks, axes)]
            landed[t, k] = together(hops) if in_step else hops
        for t in range(n):
            ready[t] = following(t, o, landed[t, k])
    return ready


def body(acts, enc_weight, enc_bias, dec_weight, dec_bias, active, counts):
    tok_dev, width = acts.shape
    lat_dev = dec_weight.shape[0]
    half = tok_dev // 2
    my_index = lax.axis_index("index")
    my_group = lax.axis_index("group")
    core = my_group % 2
    my_y = my_group // 2
    my_z = my_index // SIDE
    my_x = my_index % SIDE
    ahead = jnp.where(core == 0, 1, SIDE - 1)

    own_count = lat_dev // BLOCK
    own_blocks = my_index * own_count + jnp.arange(own_count)
    slots = jnp.arange(active.shape[1])[None, :] < counts[:, None]
    matches = (active[:, :, None] == own_blocks[None, None, :]) & slots[:, :, None]
    block_live = jnp.any(matches, axis=1).astype(F32)

    def live_rows(o2):
        o1 = jnp.arange(SIDE)
        steps_a = ((my_z + ahead * o2) % SIDE) * SIDE + (my_x + ahead * o1) % SIDE
        steps_b = ((my_z + ahead * o1) % SIDE) * SIDE + (my_x + ahead * o2) % SIDE
        live = block_live[jnp.concatenate([steps_a, steps_b])]
        return jnp.repeat(jnp.repeat(live, BLOCK, axis=1), half, axis=0)

    near_axes, far_axes = ("x", "z"), ("z", "x")
    span = SIDE // TRAINS

    def gather(blocks, direct):
        near = near_gather(blocks, near_axes, direct)
        first = [
            [jnp.concatenate(near[h][t * span : (t + 1) * span], axis=0) for h in range(2)] for t in range(TRAINS)
        ]
        pieces = {(0, t): first[t] for t in range(TRAINS)}

        def keep(t, o, landed):
            pieces[o, t] = landed
            return landed

        rings(first, keep, far_axes)
        return [[pieces[o, t][h] for h in range(2) for t in range(TRAINS)] for o in range(SIDE)]

    halves = [acts[:half], acts[half:]]
    rows = gather(halves, False)
    codes = {}
    for o2 in ARRIVAL:
        preact = jnp.dot(jnp.concatenate(rows[o2], axis=0), enc_weight, preferred_element_type=F32) + enc_bias
        codes[o2] = jnp.where(live_rows(o2) > 0.0, jnp.maximum(preact, 0.0), 0.0).astype(BF16)

    codes_all = jnp.concatenate([codes[o2] for o2 in ARRIVAL], axis=0)
    part = lat_dev // 8
    picked = []
    for other in (0, 1):
        toward = ahead if other == 0 else SIDE - ahead
        for oy in range(SIDE):
            at = ((my_y + toward * oy) % SIDE) * 2 + (core + other) % 2
            picked.append(lax.dynamic_slice_in_dim(codes_all, at * part, part, axis=1))
    codes_own = jnp.concatenate(picked[:SIDE], axis=1)
    codes_other = jnp.concatenate(picked[SIDE:], axis=1)

    partial = {}
    for o2 in (3, 2, 1, 0):
        partial[o2] = jnp.dot(codes[o2], dec_weight, preferred_element_type=F32).astype(BF16)
    n = half * span

    def own_part(t, o):
        return [partial[o][(h * TRAINS + t) * n : (h * TRAINS + t + 1) * n] for h in range(2)]

    def add_own(t, o, landed):
        return [
            (block.astype(F32) + own.astype(F32)).astype(BF16) for block, own in zip(landed, own_part(t, o - 1))
        ]

    sums = rings([own_part(t, 3) for t in range(TRAINS)], add_own, far_axes, False)
    parts = [
        [sums[t][h][i * half : (i + 1) * half] for t in range(TRAINS) for i in range(span)] for h in range(2)
    ]
    recons = [(total + dec_bias).astype(BF16) for total in near_reduce(parts, near_axes, True)]
    errors = gather(
        [(recon.astype(F32) - own.astype(F32)).astype(BF16) for recon, own in zip(recons, halves)],
        True,
    )
    error_all = jnp.concatenate([block for o2 in ARRIVAL for block in errors[o2]], axis=0)

    cols = width // TAIL
    pairs = []
    for c in range(TAIL):

        def grad_of(codes_part):
            return lax.dot_general(
                codes_part,
                error_all[:, c * cols : (c + 1) * cols],
                (((0,), (0,)), ((), ())),
                preferred_element_type=F32,
            ).astype(BF16)

        theirs = lax.ppermute(grad_of(codes_other), AXES, SWAP)
        pair = (grad_of(codes_own).astype(F32) + theirs.astype(F32)).astype(BF16)
        pairs.append([pair[o * part : (o + 1) * part] for o in range(SIDE)])

    def add_pair(t, o, landed):
        total = landed[0].astype(F32) + pairs[t][o - 1].astype(F32)
        return [total.astype(BF16)]

    grads = rings([[pair[3]] for pair in pairs], add_pair, ("y",))
    grads = [total[0].astype(F32) for total in grads]
    return jnp.concatenate(recons, axis=0), jnp.concatenate(grads, axis=1)


def solution(mesh):
    in_specs = (
        P(("group", "index"), None),
        P(None, "index"),
        P("index"),
        P("index", None),
        P(),
        P("group", None),
        P("group"),
    )
    out_specs = (P(("group", "index"), None), P(("index", "group"), None))
    return jax.shard_map(body, mesh=mesh, in_specs=in_specs, out_specs=out_specs, check_vma=False)
```
